512 devices in a mesh: grp: 16 (over z, core), ep: 32 (over y, x).
Axes of the slice: x: 4, y: 8, z: 8, core: 2. Of those that a mesh axis runs over, the one named last changes fastest.
Arguments:
- tokens: bfloat16 [65536, 2048], P(('grp', 'ep')), may hold values from -6 to 6
- out_grad: bfloat16 [65536, 2048], P(('grp', 'ep')), may hold values from -1.5 to 1.5
- routes: int32 [65536, 2], P(('grp', 'ep')), may hold values from 0 to 15, as said below
- gates: bfloat16 [65536, 2], P(('grp', 'ep')), may hold values from 0.099609375 to 1
- w_gate_up: bfloat16 [32, 2048, 1024], P('ep', 'grp'), may hold values from -0.125 to 0.125
- w_down: bfloat16 [32, 2048, 512], P('ep', 'grp'), may hold values from -0.25 to 0.25
- plan: int32 [32], replicated, may hold values from 0 to 15, as said below
- failed: int32 [16, 32], replicated, may hold values from 0 to 1, as said below
Outputs:
- token_grad: bfloat16 [65536, 2048], P(('grp', 'ep'))
- gate_grad: bfloat16 [65536, 2], P(('grp', 'ep'))
- weight_grad: float32 [16, 2048, 1536], P(None, ('grp', 'ep'))
The draws below stay inside these ranges and needn't reach their ends.
Inputs may be any that keep to these rules, and one draw needn't show every extreme that they name: `plan`: each expert is hosted by one or three slots. Each group has one to 4 failed slots, and every expert keeps a live replica in every group. A token names 2 different experts. Under the replica rule the routes of one device reach any slot at most 10 times, and in every group some slot receives exactly 10 routes from every device of the group.
All inputs are finite; a program needn't handle non-finite values.
Results may differ from the reference program's by a relative error of at most 0.0058.
Values may be sent and summed in bfloat16 or wider, within the bound.
No kernel may reach another device: no remote copies, remote signals or barrier semaphores. Data moves between devices by JAX's collectives and lax.ppermute only.
A program may use at most 128 MiB of HBM per device.

```python
import math
from functools import partial
import jax
import jax.numpy as jnp
from jax import lax

D = 2048
FF = 512
TOPK = 2
TOK_DEV = 128
EXPERTS = 16
CAP = 10
MAXFAIL = 4
TOKENS = 65536
N_GRP = 16
N_EP = 32


def layout(key):
    base_key = jax.random.fold_in(key, 4111)
    slot_order = jax.random.permutation(jax.random.fold_in(base_key, 1), N_EP)
    expert_order = jax.random.permutation(jax.random.fold_in(base_key, 2), EXPERTS)
    position = jnp.arange(N_EP)
    extra_rank = jnp.maximum(position - EXPERTS, 0)
    owners = jnp.where(position < EXPERTS, expert_order[position % EXPERTS], expert_order[extra_rank // 2])
    plan = jnp.zeros((N_EP,), jnp.int32).at[slot_order].set(owners.astype(jnp.int32))

    def group_failures(group_index):
        group_key = jax.random.fold_in(jax.random.fold_in(base_key, 3), group_index)
        fail_count = jax.random.randint(jax.random.fold_in(group_key, 1), (), 1, MAXFAIL + 1)
        extra_order = jax.random.permutation(jax.random.fold_in(group_key, 2), EXPERTS)
        dead_slots = jnp.concatenate([jnp.zeros((EXPERTS,), jnp.int32), (extra_order < fail_count).astype(jnp.int32)])
        return jnp.zeros((N_EP,), jnp.int32).at[slot_order].set(dead_slots)
    failed = jax.vmap(group_failures)(jnp.arange(N_GRP))
    full_expert = jax.random.randint(jax.random.fold_in(base_key, 4), (N_GRP,), 0, EXPERTS)
    return (plan, failed.astype(jnp.int32), full_expert)


def draw_plan(key, part):
    return layout(key)[0]


def draw_failed(key, part):
    return layout(key)[1]


def device_table(key, plan, failed, full_expert, group_index, device_index):
    entry_slot = jnp.arange(N_EP * CAP) // CAP
    entry_expert = plan[entry_slot]
    device_key = jax.random.fold_in(jax.random.fold_in(key, 5333), group_index * N_EP + device_index)
    usable = 1 - failed[group_index][entry_slot]
    priority = jnp.where(entry_expert == full_expert[group_index], 2, 1) * usable
    noise = jax.random.randint(jax.random.fold_in(device_key, 1), (N_EP * CAP,), 0, 16384)
    scores = priority * 134217728 + noise * 4096 + jnp.arange(N_EP * CAP)
    chosen = entry_expert[jnp.argsort(-scores)[:TOK_DEV * TOPK]]
    table = jnp.sort(chosen).reshape(TOPK, TOK_DEV).T
    flips = jax.random.randint(jax.random.fold_in(device_key, 2), (TOK_DEV, 1), 0, 2)
    table = jnp.where(flips == 1, table[:, ::-1], table)
    token_order = jax.random.permutation(jax.random.fold_in(device_key, 3), TOK_DEV)
    return table[token_order]


def draw_routes(key, part):
    plan, failed, full_expert = layout(key)

    def per_group(group_index):
        return jax.vmap(partial(device_table, key, plan, failed, full_expert, group_index))(jnp.arange(N_EP))
    grid = jax.vmap(per_group)(jnp.arange(N_GRP))
    return grid.reshape(TOKENS, TOPK).astype(jnp.int32)


def levels(stream_key, shape, cuts, smallest, top_value):
    gain = 1.0
    for dim, blocks in cuts:
        draws = jax.random.uniform(jax.random.fold_in(jax.random.fold_in(stream_key, 6), dim), (blocks,), jnp.float32, smallest / len(cuts), top_value / len(cuts))
        gain = gain * jnp.repeat(jnp.exp(draws), shape[dim] // blocks).reshape((-1,) + (1,) * (len(shape) - 1 - dim))
    return gain


def normal_values(key, extent, scale, reach, pieces=(), kind=jnp.bfloat16):
    values = jax.random.normal(key, extent, jnp.float32) * scale
    if len(pieces) > 0:
        values = levels(key, extent, pieces, -0.22, 0.18) * values
    return jnp.clip(values, min=-reach, max=reach).astype(kind)


def setup_inputs(seed: int = 0) -> dict:
    key_of = jax.random.split(jax.random.key(seed), 9)
    tokens = normal_values(key_of[0], (TOKENS, D), 1.0, 6.0, ((0, 512),))
    out_grad = normal_values(key_of[1], (TOKENS, D), 0.25, 1.5, ((0, 512),))
    routes = draw_routes(jax.random.fold_in(key_of[8], 71), 0)
    gates = jnp.clip(jnp.exp(math.log(1.0) - 2.306499 * jax.random.uniform(key_of[3], (TOKENS, TOPK), jnp.float32) ** levels(key_of[3], (TOKENS, TOPK), ((0, 512),), -0.2, 0.2)), 0.099609375, 1.0).astype(jnp.bfloat16)
    w_gate_up = normal_values(key_of[4], (N_EP, D, 2 * FF), D ** -0.5, 0.125, ((0, 32), (1, 16)))
    w_down = normal_values(key_of[5], (N_EP, D, FF), FF ** -0.5, 0.25, ((0, 32), (1, 16)))
    plan = draw_plan(jax.random.fold_in(key_of[8], 71), 0)
    failed = draw_failed(jax.random.fold_in(key_of[8], 71), 0)
    return dict(tokens=tokens, out_grad=out_grad, routes=routes, gates=gates, w_gate_up=w_gate_up, w_down=w_down, plan=plan, failed=failed)


def assign(route_ids, hosting, in_service, capacity, experts):
    route_count = route_ids.shape[0] * route_ids.shape[1]
    slot_count = hosting.shape[0]
    flat_routes = route_ids.reshape(route_count)
    expert_ids = jnp.arange(experts, dtype=jnp.int32)
    hosted = ((hosting[None, :] == expert_ids[:, None]) & (in_service[None, :] > 0)).astype(jnp.int32)
    replicas = jnp.sum(hosted, axis=1)
    ordinal = jnp.sum(hosted * (jnp.cumsum(hosted, axis=1) - 1), axis=0)
    expert_hot = (flat_routes[:, None] == expert_ids[None, :]).astype(jnp.int32)
    expert_rank = jnp.sum(expert_hot * (jnp.cumsum(expert_hot, axis=0) - 1), axis=1)
    route_replicas = jnp.sum(expert_hot * replicas[None, :], axis=1)
    replica_pick = expert_rank % route_replicas
    slot_hot = ((hosting[None, :] == flat_routes[:, None]) & (in_service[None, :] > 0)
                & (ordinal[None, :] == replica_pick[:, None])).astype(jnp.int32)
    slot_rank = jnp.sum(slot_hot * (jnp.cumsum(slot_hot, axis=0) - 1), axis=1)
    slot_index = jnp.sum(slot_hot * jnp.arange(slot_count, dtype=jnp.int32)[None, :], axis=1)
    return (slot_index * capacity + slot_rank).astype(jnp.int32)


def expert_rows(rows_x, rows_dy, rows_gate, full_gu, full_dn):
    hidden_width = full_dn.shape[1]
    projected = jnp.dot(rows_x, full_gu, preferred_element_type=jnp.float32)
    gate_pre = projected[:, :hidden_width]
    up_pre = projected[:, hidden_width:]
    sigmoid_a = jax.nn.sigmoid(gate_pre)
    silu_a = gate_pre * sigmoid_a
    hidden = (silu_a * up_pre).astype(jnp.bfloat16)
    upstream = jnp.dot(rows_dy, full_dn, preferred_element_type=jnp.float32)
    rebuilt = jnp.dot(hidden, full_dn.T, preferred_element_type=jnp.float32)
    gate_grad = jnp.sum(rows_dy.astype(jnp.float32) * rebuilt, axis=1).astype(jnp.bfloat16)
    gate_value = rows_gate.astype(jnp.float32)[:, None]
    hidden_grad = gate_value * upstream
    gate_delta = hidden_grad * up_pre * sigmoid_a * (1.0 + gate_pre * (1.0 - sigmoid_a))
    up_delta = hidden_grad * silu_a
    pre_grad = jnp.concatenate([gate_delta, up_delta], axis=1).astype(jnp.bfloat16)
    row_grad = jnp.dot(pre_grad, full_gu.T, preferred_element_type=jnp.float32).astype(jnp.bfloat16)
    gated_hidden = (gate_value * hidden.astype(jnp.float32)).astype(jnp.bfloat16)
    grad_gu = jnp.dot(rows_x.T, pre_grad, preferred_element_type=jnp.float32)
    grad_dn = jnp.dot(rows_dy.T, gated_hidden, preferred_element_type=jnp.float32)
    return row_grad, gate_grad, grad_gu, grad_dn


def reference(tokens, out_grad, routes, gates, w_gate_up, w_down, plan, failed):
    route_count = TOK_DEV * TOPK
    buffer_rows = N_EP * CAP
    expert_ids = jnp.arange(EXPERTS, dtype=jnp.int32)
    token_groups = tokens.reshape(N_GRP, N_EP, TOK_DEV, D)
    grad_groups = out_grad.reshape(N_GRP, N_EP, TOK_DEV, D)
    route_groups = routes.reshape(N_GRP, N_EP, TOK_DEV, TOPK)
    gate_groups = gates.reshape(N_GRP, N_EP, TOK_DEV, TOPK)

    def to_slots(array):
        shaped = array.reshape((N_EP, N_EP, CAP) + array.shape[2:])
        shaped = jnp.swapaxes(shaped, 0, 1)
        return shaped.reshape((N_EP, N_EP * CAP) + array.shape[2:])

    def group_step(running, inputs):
        group_tokens, group_grads, group_routes, group_gates, group_failed = inputs
        in_service = 1 - group_failed
        positions = jax.vmap(lambda route_ids: assign(route_ids, plan, in_service, CAP, EXPERTS))(group_routes)

        def pack(slot_pos, dev_tokens, dev_grads, dev_gates):
            source = jnp.full((buffer_rows,), route_count, jnp.int32).at[slot_pos].set(
                jnp.arange(route_count, dtype=jnp.int32))
            token_of = (source // TOPK).astype(jnp.int32)
            zero_row = jnp.zeros((1, D), jnp.bfloat16)
            rows_x = jnp.concatenate([dev_tokens, zero_row], axis=0)[token_of]
            rows_dy = jnp.concatenate([dev_grads, zero_row], axis=0)[token_of]
            rows_gate = jnp.concatenate([dev_gates.reshape(route_count), jnp.zeros((1,), jnp.bfloat16)])[source]
            return rows_x, rows_dy, rows_gate

        packed_x, packed_dy, packed_gate = jax.vmap(pack)(positions, group_tokens, group_grads, group_gates)

        def per_slot(operands):
            return expert_rows(*operands)

        row_grads, gate_rows, grad_gu, grad_dn = lax.map(
            per_slot, (to_slots(packed_x), to_slots(packed_dy), to_slots(packed_gate), w_gate_up, w_down))
        slot_grad = jnp.concatenate([grad_gu, grad_dn], axis=2).astype(jnp.bfloat16)
        hosted = ((plan[None, :] == expert_ids[:, None]) & (in_service[None, :] > 0)).astype(jnp.float32)
        group_grad = jnp.einsum("es,sdc->edc", hosted, slot_grad.astype(jnp.float32))
        running = running + group_grad
        back_x = to_slots(row_grads)
        back_gate = to_slots(gate_rows)

        def unpack(slot_pos, dev_back_x, dev_back_gate):
            gathered = dev_back_x[slot_pos].reshape(TOK_DEV, TOPK, D).astype(jnp.float32)
            summed = jnp.sum(gathered, axis=1).astype(jnp.bfloat16)
            return summed, dev_back_gate[slot_pos].reshape(TOK_DEV, TOPK)

        group_dx, group_dg = jax.vmap(unpack)(positions, back_x, back_gate)
        return running, (group_dx, group_dg)

    initial = jnp.zeros((EXPERTS, D, 3 * FF), jnp.float32)
    final, outputs = lax.scan(group_step, initial,
                              (token_groups, grad_groups, route_groups, gate_groups, failed))
    token_grad = outputs[0].reshape(TOKENS, D)
    gate_grad = outputs[1].reshape(TOKENS, TOPK)
    return token_grad, gate_grad, final / N_GRP
```

```python
import functools

import jax
import jax.numpy as jnp
from jax import lax
from jax.experimental import pallas as pl
from jax.experimental.pallas import tpu as pltpu
from jax.sharding import PartitionSpec as P

BF = jnp.bfloat16
F32 = jnp.float32
LANES = 128
MAIN = 8
VMEM_BYTES = 56 * 2**20
TN = (((0,), (0,)), ((), ()))
NT = (((1,), (1,)), ((), ()))


def mm(a, b, dims=(((1,), (0,)), ((), ()))):
    return lax.dot_general(a, b, dims, preferred_element_type=F32)


def iota(shape, dim):
    return lax.broadcasted_iota(jnp.int32, shape, dim)


def one_hot(cond):
    return jnp.where(cond, 1.0, 0.0).astype(BF)


def call(kernel, outs, name, **kw):
    return pl.pallas_call(
        kernel,
        out_shape=outs,
        name=name,
        compiler_params=pltpu.CompilerParams(vmem_limit_bytes=VMEM_BYTES),
        **kw,
    )


def pack_kernel(group, routes, gates, plan, failed, tokens, grads, sent, places):
    tok_count, width = tokens.shape
    slots = plan.shape[1]
    half = width // 2
    rows = slots * MAIN
    in_group = iota(failed.shape, 0) == group[0]
    dead = jnp.sum(jnp.where(in_group, failed[...], 0), axis=0, keepdims=True)
    slot_ids = iota((tok_count, slots), 1).astype(F32)
    before_slot = one_hot(iota((slots, slots), 0) < iota((slots, slots), 1))
    before_tok = one_hot(iota((tok_count, tok_count), 1) < iota((tok_count, tok_count), 0))
    experts = iota((tok_count, LANES), 1)
    ids = [routes[:, k : k + 1] for k in range(2)]
    hot = [jnp.where(experts == i, 1.0, 0.0) for i in ids]
    prefix = mm(before_tok, (hot[0] + hot[1]).astype(BF))
    rank = [
        jnp.sum(hot[0] * prefix, axis=1, keepdims=True),
        jnp.sum(hot[1] * (prefix + hot[0]), axis=1, keepdims=True),
    ]
    chosen = []
    for k in range(2):
        cand = jnp.where((plan[...] == ids[k]) & (dead == 0), 1.0, 0.0)
        ordinal = mm(cand.astype(BF), before_slot)
        count = jnp.maximum(jnp.sum(cand, axis=1, keepdims=True), 1.0)
        pick = rank[k] - count * jnp.floor((rank[k] + 0.5) / count)
        chosen.append(jnp.where(ordinal == pick, cand, 0.0))
    prefix = mm(before_tok, (chosen[0] + chosen[1]).astype(BF))
    position = [
        jnp.sum(chosen[0] * prefix, axis=1, keepdims=True),
        jnp.sum(chosen[1] * (prefix + chosen[0]), axis=1, keepdims=True),
    ]
    row_ids = iota((tok_count, rows), 1)
    lane = iota((tok_count, LANES), 1)
    main, rest, noted = [], [], jnp.zeros((tok_count, LANES), jnp.int32)
    for k in range(2):
        slot = jnp.sum(chosen[k] * slot_ids, axis=1, keepdims=True).astype(jnp.int32)
        pos = position[k].astype(jnp.int32)
        main.append(jnp.where(pos < MAIN, slot * MAIN + pos, -64))
        rest.append(jnp.where(pos < MAIN, -64, slot * MAIN + pos - MAIN))
        noted = jnp.where(lane == k, main[k], noted)
        noted = jnp.where(lane == 2 + k, rest[k], noted)
    places[...] = noted

    def pick_rows(at, shift=0):
        return one_hot((at[0] + shift == row_ids) | (at[1] + shift == row_ids))

    whole = pick_rows(main)
    sent[:, :width] = mm(whole, tokens[...], TN).astype(BF)
    sent[:, width : 2 * width] = mm(whole, grads[...], TN).astype(BF)
    cut = mm(pick_rows(rest), tokens[:, :half], TN)
    cut += mm(pick_rows(rest, 4), tokens[:, half:], TN)
    cut += mm(pick_rows(rest, 2), grads[:, :half], TN)
    cut += mm(pick_rows(rest, 6), grads[:, half:], TN)
    sent[:, 2 * width : 2 * width + half] = cut.astype(BF)
    gate_rows = jnp.zeros((rows, LANES), F32)
    for k in range(2):
        gate = jnp.broadcast_to(gates[:, k : k + 1].astype(F32), (tok_count, LANES))
        first = jnp.where(lane == 0, gate, 0.0).astype(BF)
        second = jnp.where(lane == 1, gate, 0.0).astype(BF)
        gate_rows += mm(one_hot(main[k] == row_ids), first, TN)
        gate_rows += mm(one_hot(rest[k] == row_ids), second, TN)
    sent[:, 2 * width + half :] = gate_rows.astype(BF)


def slot_kernel(got, weights, slot_grad, pre_out, gate_out, x_all, dy_all):
    rows = got.shape[0]
    width = weights.shape[0]
    hidden_width = weights.shape[1] // 3
    half = width // 2
    extra = rows // MAIN * 2
    source = iota((extra, rows), 0)
    base = source // 2 * MAIN + source % 2
    column = iota((extra, rows), 1)
    cut = got[:, 2 * width : 2 * width + half]
    first = one_hot(column == base)
    x_all[:rows] = got[:, :width]
    dy_all[:rows] = got[:, width : 2 * width]
    x_all[rows:, :half] = mm(first, cut).astype(BF)
    x_all[rows:, half:] = mm(one_hot(column == base + 4), cut).astype(BF)
    dy_all[rows:, :half] = mm(one_hot(column == base + 2), cut).astype(BF)
    dy_all[rows:, half:] = mm(one_hot(column == base + 6), cut).astype(BF)
    gate_block = got[:, 2 * width + half :]
    gate = jnp.concatenate(
        [gate_block[:, 0:1].astype(F32), mm(first, gate_block)[:, 1:2]], axis=0
    )
    pre = mm(x_all[...], weights[:, : 2 * hidden_width])
    a = pre[:, :hidden_width]
    b = pre[:, hidden_width:]
    sig = jax.nn.sigmoid(a)
    silu = a * sig
    hidden = (silu * b).astype(BF)
    hidden32 = hidden.astype(F32)
    upstream = mm(dy_all[...], weights[:, 2 * hidden_width :])
    gate_grad = jnp.sum(upstream * hidden32, axis=1, keepdims=True)
    gate_out[...] = jnp.broadcast_to(gate_grad, gate_out.shape).astype(BF)
    hidden_grad = gate * upstream
    pre_out[:, :hidden_width] = (hidden_grad * b * sig * (1.0 + a * (1.0 - sig))).astype(BF)
    pre_out[:, hidden_width:] = (hidden_grad * silu).astype(BF)
    gated = (gate * hidden32).astype(BF)
    step = 256
    for d in range(0, width, step):
        grad = mm(x_all[:, d : d + step], pre_out[...], TN)
        slot_grad[d : d + step, : 2 * hidden_width] = grad.astype(BF)
        grad = mm(dy_all[:, d : d + step], gated, TN)
        slot_grad[d : d + step, 2 * hidden_width :] = grad.astype(BF)


def back_kernel(pre_grad, gate_grad, weights, back):
    total, columns = pre_grad.shape
    width = weights.shape[0]
    rows = back.shape[0]
    extra = total - rows
    quarter = width // 4
    row = iota((rows, extra), 0)
    column = iota((rows, extra), 1)
    target = row // MAIN * 2 + row % 2
    part = row % MAIN // 2
    cut = jnp.zeros((rows, quarter), F32)
    for h in range(4):
        cols = slice(h * quarter, (h + 1) * quarter)
        grad = mm(pre_grad[...], weights[cols, :columns], NT).astype(BF)
        back[:, cols] = grad[:rows]
        cut += mm(one_hot((column == target) & (part == h)), grad[rows:])
    back[:, width : width + quarter] = cut.astype(BF)
    lane = iota((rows, LANES), 1)
    spread = mm(one_hot((column == target) & (part == 0)), gate_grad[rows:])
    gate_rows = jnp.where(lane == 0, gate_grad[:rows].astype(F32), spread)
    back[:, width + quarter :] = jnp.where(lane < 2, gate_rows, 0.0).astype(BF)


def join_kernel(back, places, token_grad, gate_grad):
    tok_count, width = token_grad.shape
    rows = back.shape[0]
    quarter = width // 4
    row_ids = iota((tok_count, rows), 1)
    main = [places[:, k : k + 1] for k in range(2)]
    rest = [places[:, 2 + k : 3 + k] for k in range(2)]
    whole = one_hot((main[0] == row_ids) | (main[1] == row_ids))
    cut = back[:, width : width + quarter]
    for h in range(4):
        cols = slice(h * quarter, (h + 1) * quarter)
        here = one_hot((rest[0] + 2 * h == row_ids) | (rest[1] + 2 * h == row_ids))
        token_grad[:, cols] = (mm(whole, back[:, cols]) + mm(here, cut)).astype(BF)
    gate_rows = back[:, width + quarter :]
    for k in range(2):
        value = mm(one_hot(main[k] == row_ids), gate_rows)[:, 0:1]
        value += mm(one_hot(rest[k] == row_ids), gate_rows)[:, 1:2]
        gate_grad[:, k : k + 1] = value.astype(BF)


def expert_kernel(groups, plan, mixed, out):
    out[...] = jnp.zeros_like(out)
    for s in range(mixed.shape[0]):
        e = plan[s]
        out[e] += mixed[s].astype(F32)
    out[...] = out[...] * (1.0 / groups)


def local(tokens, out_grad, routes, gates, w_gate_up, w_down, plan, failed):
    groups = lax.axis_size("grp")
    slots = lax.axis_size("ep")
    tok_count, width = tokens.shape
    hidden_width = w_down.shape[2]
    experts = slots // 2
    rows = slots * MAIN
    total = slots * (MAIN + 2)
    smem = pl.BlockSpec(memory_space=pltpu.SMEM)
    vmem = pl.BlockSpec(memory_space=pltpu.VMEM)
    weights = jnp.concatenate([w_gate_up[0], w_down[0]], axis=1)
    weights = lax.all_gather(weights, "grp", axis=0, tiled=True)
    sent, places = call(
        pack_kernel,
        (
            jax.ShapeDtypeStruct((rows, 2 * width + width // 2 + LANES), BF),
            jax.ShapeDtypeStruct((tok_count, LANES), jnp.int32),
        ),
        "pack",
        in_specs=[smem] + [vmem] * 6,
    )(
        lax.axis_index("grp").reshape(1),
        routes,
        gates,
        plan.reshape(1, slots),
        failed,
        tokens,
        out_grad,
    )
    got = lax.all_to_all(sent, "ep", split_axis=0, concat_axis=0, tiled=True)
    slot_grad, pre_grad, gate_rows = call(
        slot_kernel,
        (
            jax.ShapeDtypeStruct((width, 3 * hidden_width), BF),
            jax.ShapeDtypeStruct((total, 2 * hidden_width), BF),
            jax.ShapeDtypeStruct((total, LANES), BF),
        ),
        "slot",
        scratch_shapes=[pltpu.VMEM((total, width), BF)] * 2,
    )(got, weights)
    owned = lax.psum_scatter(slot_grad, "grp", scatter_dimension=0, tiled=True)
    back = call(
        back_kernel,
        jax.ShapeDtypeStruct((rows, width + width // 4 + LANES), BF),
        "back",
    )(pre_grad, gate_rows, weights)
    back = lax.all_to_all(back, "ep", split_axis=0, concat_axis=0, tiled=True)
    token_grad, gate_grad = call(
        join_kernel,
        (
            jax.ShapeDtypeStruct((tok_count, width), BF),
            jax.ShapeDtypeStruct((tok_count, 2), BF),
        ),
        "join",
    )(back, places)
    each = owned.shape[0] // slots
    owned = owned.reshape(slots, each, 3 * hidden_width)
    mixed = lax.all_to_all(owned, "ep", split_axis=0, concat_axis=0, tiled=True)
    weight_grad = call(
        functools.partial(expert_kernel, groups),
        jax.ShapeDtypeStruct((experts, each, 3 * hidden_width), F32),
        "experts",
        in_specs=[smem, vmem],
    )(plan, mixed)
    return token_grad, gate_grad, weight_grad


def solution(mesh):
    placed = (
        P(("grp", "ep"), None),
        P(("grp", "ep"), None),
        P(("grp", "ep"), None),
        P(("grp", "ep"), None),
        P("ep", "grp", None),
        P("ep", "grp", None),
        P(),
        P(),
    )
    return jax.shard_map(
        local,
        mesh=mesh,
        in_specs=placed,
        out_specs=(P(("grp", "ep"), None), P(("grp", "ep"), None), P(None, ("grp", "ep"), None)),
        check_vma=False,
    )
```

```python
import functools

import jax
import jax.numpy as jnp
from jax import lax
from jax.experimental import pallas as pl
from jax.experimental.pallas import tpu as pltpu
from jax.sharding import PartitionSpec as P

BF = jnp.bfloat16
F32 = jnp.float32
LANES = 128
MAIN = 8
TN = (((0,), (0,)), ((), ()))
NT = (((1,), (1,)), ((), ()))


def mm(a, b, dims=(((1,), (0,)), ((), ()))):
    return lax.dot_general(a, b, dims, preferred_element_type=F32)


def iota(shape, dim):
    return lax.broadcasted_iota(jnp.int32, shape, dim)


def one_hot(cond):
    return jnp.where(cond, 1.0, 0.0).astype(BF)


def call(kernel, outs, name, mib, **kw):
    return pl.pallas_call(
        kernel,
        out_shape=outs,
        name=name,
        compiler_params=pltpu.CompilerParams(vmem_limit_bytes=mib * 2**20),
        **kw,
    )


ORDER = (-4, -2, 3, -3, 2, -1, 1, 0)
FIRST = 3


def feature_blocks(place, chips):
    blocks = []
    for core in (place[1], 1 - place[1]):
        for shift in ORDER:
            chip = lax.rem(place[0] + (1 - 2 * core) * shift + chips, chips)
            blocks.append(pl.ds(pl.multiple_of((2 * chip + core) * LANES, LANES), LANES))
    return blocks


def pack_kernel(place, routes, gates, plan, failed, tokens_in, grads_in, sent, places, tokens, grads):
    tok_count, width = tokens.shape
    slots = plan.shape[1]
    half = width // 2
    rows = slots * MAIN
    for j, block in enumerate(feature_blocks(place, width // (2 * LANES))):
        cols = slice(j * LANES, (j + 1) * LANES)
        tokens[:, cols] = tokens_in[:, block]
        grads[:, cols] = grads_in[:, block]
    in_group = iota(failed.shape, 0) == 2 * place[0] + place[1]
    dead = jnp.sum(jnp.where(in_group, failed[...], 0), axis=0, keepdims=True)
    hosting = jnp.where(dead == 0, plan[...], -1)
    diagonal = iota((slots, slots), 0) == iota((slots, slots), 1)
    hosting = jnp.sum(jnp.where(diagonal, hosting, 0), axis=1, keepdims=True)
    slot_ids = iota((slots, tok_count), 0).astype(F32)
    before_slot = one_hot(iota((slots, slots), 1) < iota((slots, slots), 0))
    before_tok = one_hot(iota((tok_count, tok_count), 0) < iota((tok_count, tok_count), 1))
    experts = iota((slots, tok_count), 0)
    ids = [routes[k : k + 1, :] for k in range(2)]
    hot = [jnp.where(experts == i, 1.0, 0.0) for i in ids]
    prefix = mm((hot[0] + hot[1]).astype(BF), before_tok)
    rank = [
        jnp.sum(hot[0] * prefix, axis=0, keepdims=True),
        jnp.sum(hot[1] * (prefix + hot[0]), axis=0, keepdims=True),
    ]
    chosen = []
    for k in range(2):
        cand = jnp.where(hosting == ids[k], 1.0, 0.0)
        ordinal = mm(before_slot, cand.astype(BF))
        count = jnp.maximum(jnp.sum(cand, axis=0, keepdims=True), 1.0)
        pick = rank[k] - count * jnp.floor((rank[k] + 0.5) / count)
        chosen.append(jnp.where(ordinal == pick, cand, 0.0))
    prefix = mm((chosen[0] + chosen[1]).astype(BF), before_tok)
    position = [
        jnp.sum(chosen[0] * prefix, axis=0, keepdims=True),
        jnp.sum(chosen[1] * (prefix + chosen[0]), axis=0, keepdims=True),
    ]
    row_ids = iota((rows, tok_count), 0)
    main, rest = [], []
    for k in range(2):
        slot = jnp.sum(chosen[k] * slot_ids, axis=0, keepdims=True).astype(jnp.int32)
        pos = position[k].astype(jnp.int32)
        main.append(jnp.where(pos < MAIN, slot * MAIN + pos, -64))
        rest.append(jnp.where(pos < MAIN, -64, slot * MAIN + pos - MAIN))
    line = iota(places.shape, 0)
    noted = jnp.full(places.shape, -64, jnp.int32)
    for i, at in enumerate(main + rest):
        noted = jnp.where(line == i, at, noted)
    places[...] = noted

    def pick_rows(at, shift=0):
        return one_hot((at[0] + shift == row_ids) | (at[1] + shift == row_ids))

    whole = pick_rows(main)
    sent[:, :width] = mm(whole, tokens[...]).astype(BF)
    sent[:, width : 2 * width] = mm(whole, grads[...]).astype(BF)
    cut = mm(pick_rows(rest), tokens[:, :half])
    cut += mm(pick_rows(rest, 4), tokens[:, half:])
    cut += mm(pick_rows(rest, 2), grads[:, :half])
    cut += mm(pick_rows(rest, 6), grads[:, half:])
    sent[:, 2 * width : 2 * width + half] = cut.astype(BF)
    lane_ids = iota((LANES, tok_count), 0)
    gate_rows = jnp.zeros((rows, LANES), F32)
    for k in range(2):
        gate = gates[k : k + 1, :].astype(F32)
        first = jnp.where(lane_ids == 0, gate, 0.0).astype(BF)
        second = jnp.where(lane_ids == 1, gate, 0.0).astype(BF)
        gate_rows += mm(one_hot(main[k] == row_ids), first, NT)
        gate_rows += mm(one_hot(rest[k] == row_ids), second, NT)
    sent[:, 2 * width + half :] = gate_rows.astype(BF)


def stack_kernel(*refs):
    out = refs[-1]
    at = 0
    for ref in refs[:-1]:
        out[at : at + ref.shape[0]] = ref[...]
        at += ref.shape[0]


def stack(blocks):
    rows, columns = sum(b.shape[0] for b in blocks), blocks[0].shape[1]
    return call(
        stack_kernel,
        jax.ShapeDtypeStruct((rows, columns), BF),
        "stack",
        8,
        cost_estimate=pl.CostEstimate(flops=0, bytes_accessed=2 * rows * columns, transcendentals=0),
    )(*blocks)


def slot_kernel(got, w0, w1, w2, w3, mine, first, later, pre_out, gate_out, x_all, dy_all):
    rows = got.shape[0]
    hidden_width = w0.shape[1] // 3
    half = w0.shape[0] + w1.shape[0]
    width = 2 * half
    extra = rows // MAIN * 2
    source = iota((extra, rows), 0)
    base = source // 2 * MAIN + source % 2
    column = iota((extra, rows), 1)
    cut = got[:, 2 * width : 2 * width + half]
    head = one_hot(column == base)
    x_all[:rows] = got[:, :width]
    x_all[rows:, :half] = mm(head, cut).astype(BF)
    x_all[rows:, half:] = mm(one_hot(column == base + 4), cut).astype(BF)
    dy_all[:rows] = got[:, width : 2 * width]
    dy_all[rows:, :half] = mm(one_hot(column == base + 2), cut).astype(BF)
    dy_all[rows:, half:] = mm(one_hot(column == base + 6), cut).astype(BF)
    gate_block = got[:, 2 * width + half :]
    gate = jnp.concatenate(
        [gate_block[:, 0:1].astype(F32), mm(head, gate_block)[:, 1:2]], axis=0
    )
    wide = slice(0, 2 * hidden_width)
    down = slice(2 * hidden_width, 3 * hidden_width)
    pre, upstream, at = 0.0, 0.0, 0
    for w in (w0, w1, w2, w3):
        cols = slice(at, at + w.shape[0])
        pre += mm(x_all[:, cols], w[:, wide])
        upstream += mm(dy_all[:, cols], w[:, down])
        at += w.shape[0]
    a = pre[:, :hidden_width]
    b = pre[:, hidden_width:]
    sig = jax.nn.sigmoid(a)
    silu = a * sig
    hidden32 = (silu * b).astype(BF).astype(F32)
    gate_grad = jnp.sum(upstream * hidden32, axis=1, keepdims=True)
    gate_out[...] = jnp.broadcast_to(gate_grad, gate_out.shape).astype(BF)
    hidden_grad = gate * upstream
    pre_out[:, :hidden_width] = (hidden_grad * b * sig * (1.0 + a * (1.0 - sig))).astype(BF)
    pre_out[:, hidden_width:] = (hidden_grad * silu).astype(BF)
    gated = (gate * hidden32).astype(BF)
    at = half
    for out in (first, later, mine):
        at = 0 if out is mine else at
        for d in range(0, out.shape[0], LANES):
            cols = slice(at, at + LANES)
            out[d : d + LANES, wide] = mm(x_all[:, cols], pre_out[...], TN).astype(BF)
            out[d : d + LANES, down] = mm(dy_all[:, cols], gated, TN).astype(BF)
            at += LANES


def back_kernel(pre_grad, gate_grad, w0, w1, w2, w3, back, cut_rows):
    total, columns = pre_grad.shape
    width = 2 * (w0.shape[0] + w1.shape[0])
    rows = back.shape[0]
    extra = total - rows
    quarter = width // 4
    at = 0
    for w in (w0, w1, w2, w3):
        grad = mm(pre_grad[...], w[:, :columns], NT).astype(BF)
        back[:, at : at + w.shape[0]] = grad[:rows]
        cut_rows[:, at : at + w.shape[0]] = grad[rows:]
        at += w.shape[0]
    row = iota((rows, extra), 0)
    column = iota((rows, extra), 1)
    target = row // MAIN * 2 + row % 2
    part = row % MAIN // 2
    cut = jnp.zeros((rows, quarter), F32)
    for h in range(4):
        cols = slice(h * quarter, (h + 1) * quarter)
        cut += mm(one_hot((column == target) & (part == h)), cut_rows[:, cols])
    back[:, width : width + quarter] = cut.astype(BF)
    lane = iota((rows, LANES), 1)
    spread = mm(one_hot((column == target) & (part == 0)), gate_grad[rows:])
    gate_rows = jnp.where(lane == 0, gate_grad[:rows].astype(F32), spread)
    back[:, width + quarter :] = jnp.where(lane < 2, gate_rows, 0.0).astype(BF)


def join_kernel(place, back, places, token_grad, gate_grad):
    tok_count, width = token_grad.shape
    rows = back.shape[0]
    quarter = width // 4
    row_ids = iota((rows, tok_count), 0)
    main = [places[k : k + 1, :] for k in range(2)]
    rest = [places[2 + k : 3 + k, :] for k in range(2)]
    whole = one_hot((main[0] == row_ids) | (main[1] == row_ids))
    cut = back[:, width : width + quarter]
    blocks = feature_blocks(place, width // (2 * LANES))
    for h in range(4):
        cols = slice(h * quarter, (h + 1) * quarter)
        here = one_hot((rest[0] + 2 * h == row_ids) | (rest[1] + 2 * h == row_ids))
        total = mm(whole, back[:, cols], TN) + mm(here, cut, TN)
        for j in range(quarter // LANES):
            block = blocks[h * (quarter // LANES) + j]
            token_grad[:, block] = total[:, j * LANES : (j + 1) * LANES].astype(BF)
    gate_rows = back[:, width + quarter :]
    for k in range(2):
        value = mm(gate_rows, one_hot(main[k] == row_ids), TN)[0:1, :]
        value += mm(gate_rows, one_hot(rest[k] == row_ids), TN)[1:2, :]
        gate_grad[k : k + 1, :] = value.astype(BF)


def expert_kernel(groups, plan, mixed, out):
    out[...] = jnp.zeros_like(out)
    for s in range(mixed.shape[0]):
        e = plan[s]
        out[e] += mixed[s].astype(F32)
    out[...] = out[...] * (1.0 / groups)


def move(array, step):
    chips = lax.axis_size("z")
    pairs = []
    for z in range(chips):
        pairs.append((2 * z, 2 * ((z + step) % chips)))
        pairs.append((2 * z + 1, 2 * ((z - step) % chips) + 1))
    return lax.ppermute(array, ("z", "core"), pairs)


def swap(array):
    return lax.ppermute(array, "core", [(0, 1), (1, 0)])


def local(tokens, out_grad, routes, gates, w_gate_up, w_down, plan, failed):
    chips = lax.axis_size("z")
    groups = chips * 2
    slots = lax.axis_size("ep")
    tok_count, width = tokens.shape
    hidden_width = w_down.shape[2]
    columns = 3 * hidden_width
    experts = slots // 2
    rows = slots * MAIN
    total = slots * (MAIN + 2)
    each = width // (groups * slots)
    smem = pl.BlockSpec(memory_space=pltpu.SMEM)
    vmem = pl.BlockSpec(memory_space=pltpu.VMEM)
    place = jnp.stack([lax.axis_index("z"), lax.axis_index("core")])

    sent, places = call(
        pack_kernel,
        (
            jax.ShapeDtypeStruct((rows, 2 * width + width // 2 + LANES), BF),
            jax.ShapeDtypeStruct((8, tok_count), jnp.int32),
        ),
        "pack",
        56,
        in_specs=[smem] + [vmem] * 6,
        scratch_shapes=[pltpu.VMEM((tok_count, width), BF)] * 2,
    )(
        place,
        routes.T,
        gates.T,
        plan.reshape(1, slots),
        failed,
        tokens,
        out_grad,
    )
    sent, w_gate_up, w_down = lax.optimization_barrier((sent, w_gate_up, w_down))
    got = lax.all_to_all(sent, "ep", split_axis=0, concat_axis=0, tiled=True)
    own = jnp.concatenate([w_gate_up[0], w_down[0]], axis=1)
    below, above = move(own, 1), move(own, -1)
    third, above2 = move(below, 2), move(above, -1)
    last, above3 = move(stack([third, below]), 1), move(above2, -1)
    w_mine = [stack([last, above3]), stack([third, above2, below, above, own])]
    w_all = w_mine + [swap(w) for w in w_mine]

    part = width // groups
    mine, first, later, pre_grad, gate_rows = call(
        slot_kernel,
        (
            jax.ShapeDtypeStruct((width // 2, columns), BF),
            jax.ShapeDtypeStruct((FIRST * part, columns), BF),
            jax.ShapeDtypeStruct((width // 2 - FIRST * part, columns), BF),
            jax.ShapeDtypeStruct((total, 2 * hidden_width), BF),
            jax.ShapeDtypeStruct((total, LANES), BF),
        ),
        "slot",
        32,
        in_specs=[vmem] * 5,
        scratch_shapes=[pltpu.VMEM((total, width), BF)] * 2,
    )(got, *w_all)
    first, later = swap(first), swap(later)
    back = call(
        back_kernel,
        jax.ShapeDtypeStruct((rows, width + width // 4 + LANES), BF),
        "back",
        24,
        in_specs=[vmem] * 6,
        scratch_shapes=[pltpu.VMEM((total - rows, width), BF)],
    )(pre_grad, gate_rows, *w_all)

    def both(j, n=1):
        theirs, at = (first, j) if j < FIRST else (later, j - FIRST)
        return (
            mine[j * part : (j + n) * part].astype(F32)
            + theirs[at * part : (at + n) * part].astype(F32)
        )

    minus, plus = both(0, 2).astype(BF), both(2).astype(BF)
    minus, plus, back = lax.optimization_barrier((minus, plus, back))
    minus, plus = move(minus, -1), move(plus, 1)
    far_sum = (minus[:part].astype(F32) + both(3)).astype(BF)
    plus = (plus.astype(F32) + both(4)).astype(BF)
    far_sum, plus = move(far_sum, -2), move(plus, 1)
    minus = (far_sum.astype(F32) + minus[part:].astype(F32) + both(5)).astype(BF)
    plus = (plus.astype(F32) + both(6)).astype(BF)
    minus, plus = move(minus, -1), move(plus, 1)
    owned = (minus.astype(F32) + plus.astype(F32) + both(7)).astype(BF)

    back = lax.all_to_all(back, "ep", split_axis=0, concat_axis=0, tiled=True)
    owned, back = lax.optimization_barrier((owned, back))
    token_grad, gate_grad = call(
        join_kernel,
        (
            jax.ShapeDtypeStruct((tok_count, width), BF),
            jax.ShapeDtypeStruct((2, tok_count), BF),
        ),
        "join",
        16,
        in_specs=[smem, vmem, vmem],
    )(place, back, places)
    owned = owned.reshape(slots, each, columns)
    mixed = lax.all_to_all(owned, "ep", split_axis=0, concat_axis=0, tiled=True)
    weight_grad = call(
        functools.partial(expert_kernel, groups),
        jax.ShapeDtypeStruct((experts, each, columns), F32),
        "experts",
        8,
        in_specs=[smem, vmem],
    )(plan, mixed)
    return token_grad, gate_grad.T, weight_grad


def solution(mesh):
    devices = mesh.devices.reshape(mesh.shape["grp"] // 2, 2, mesh.shape["ep"])
    fine = jax.sharding.Mesh(devices, ("z", "core", "ep"))
    everywhere = P(("z", "core", "ep"), None)
    weight = P("ep", ("z", "core"), None)
    return jax.shard_map(
        local,
        mesh=fine,
        in_specs=(everywhere,) * 4 + (weight, weight, P(), P()),
        out_specs=(everywhere, everywhere, P(None, ("z", "core", "ep"), None)),
        check_vma=False,
    )
```

```python
import functools

import jax
import jax.numpy as jnp
from jax import lax
from jax.experimental import pallas as pl
from jax.experimental.pallas import tpu as pltpu
from jax.sharding import PartitionSpec as P

BF = jnp.bfloat16
F32 = jnp.float32
LANES = 128
MAIN = 8
TN = (((0,), (0,)), ((), ()))
NT = (((1,), (1,)), ((), ()))


def mm(a, b, dims=(((1,), (0,)), ((), ()))):
    return lax.dot_general(a, b, dims, preferred_element_type=F32)


def iota(shape, dim):
    return lax.broadcasted_iota(jnp.int32, shape, dim)


def one_hot(cond):
    return jnp.where(cond, 1.0, 0.0).astype(BF)


def call(kernel, outs, name, mib, **kw):
    return pl.pallas_call(
        kernel,
        out_shape=outs,
        name=name,
        compiler_params=pltpu.CompilerParams(vmem_limit_bytes=mib * 2**20),
        **kw,
    )


ORDER = (-4, -2, 3, -3, 2, -1, 1, 0)
FIRST = 3


def feature_blocks(place, chips):
    blocks = []
    z, mine = place[0][0], place[1][0]
    for core in (mine, 1 - mine):
        for shift in ORDER:
            chip = lax.rem(z + (1 - 2 * core) * shift + chips, chips)
            blocks.append(pl.ds(pl.multiple_of((2 * chip + core) * LANES, LANES), LANES))
    return blocks


def pack_kernel(
    z, core, routes, gates, plan, failed, tokens_in, grads_in, sent, places, *scratch
):
    whole_in, whole, packed, in_sems, out_sems = scratch
    tok_count, width = tokens_in.shape
    slots = plan.shape[1]
    half = width // 2
    rows = slots * MAIN
    loads = []
    for i, ref in enumerate((tokens_in, grads_in)):
        loads.append(pltpu.make_async_copy(ref, whole_in.at[i], in_sems.at[i]))
        loads[i].start()
    in_group = iota(failed.shape, 0) == 2 * z[0] + core[0]
    dead = jnp.sum(jnp.where(in_group, failed[...], 0), axis=0, keepdims=True)
    hosting = jnp.where(dead == 0, plan[...], -1)
    diagonal = iota((slots, slots), 0) == iota((slots, slots), 1)
    hosting = jnp.sum(jnp.where(diagonal, hosting, 0), axis=1, keepdims=True)
    slot_ids = iota((slots, tok_count), 0).astype(F32)
    before_slot = one_hot(iota((slots, slots), 1) < iota((slots, slots), 0))
    before_tok = one_hot(iota((tok_count, tok_count), 0) < iota((tok_count, tok_count), 1))
    experts = iota((slots, tok_count), 0)
    ids = [routes[k : k + 1, :] for k in range(2)]
    hot = [jnp.where(experts == i, 1.0, 0.0) for i in ids]
    prefix = mm((hot[0] + hot[1]).astype(BF), before_tok)
    rank = [
        jnp.sum(hot[0] * prefix, axis=0, keepdims=True),
        jnp.sum(hot[1] * (prefix + hot[0]), axis=0, keepdims=True),
    ]
    chosen = []
    for k in range(2):
        cand = jnp.where(hosting == ids[k], 1.0, 0.0)
        ordinal = mm(before_slot, cand.astype(BF))
        count = jnp.maximum(jnp.sum(cand, axis=0, keepdims=True), 1.0)
        pick = rank[k] - count * jnp.floor((rank[k] + 0.5) / count)
        chosen.append(jnp.where(ordinal == pick, cand, 0.0))
    prefix = mm((chosen[0] + chosen[1]).astype(BF), before_tok)
    position = [
        jnp.sum(chosen[0] * prefix, axis=0, keepdims=True),
        jnp.sum(chosen[1] * (prefix + chosen[0]), axis=0, keepdims=True),
    ]
    row_ids = iota((rows, tok_count), 0)
    main, rest = [], []
    for k in range(2):
        slot = jnp.sum(chosen[k] * slot_ids, axis=0, keepdims=True).astype(jnp.int32)
        pos = position[k].astype(jnp.int32)
        main.append(jnp.where(pos < MAIN, slot * MAIN + pos, -64))
        rest.append(jnp.where(pos < MAIN, -64, slot * MAIN + pos - MAIN))
    line = iota(places.shape, 0)
    noted = jnp.full(places.shape, -64, jnp.int32)
    for i, at in enumerate(main + rest):
        noted = jnp.where(line == i, at, noted)
    places[...] = noted

    def pick_rows(at, shift=0):
        return one_hot((at[0] + shift == row_ids) | (at[1] + shift == row_ids))

    stores = []

    def store(i, at):
        stores.append(pltpu.make_async_copy(packed.at[:, at], sent.at[:, at], out_sems.at[i]))
        stores[i].start()

    blocks = feature_blocks((z, core), width // (2 * LANES))
    picked = pick_rows(main)
    for i in range(2):
        loads[i].wait()
        for j, block in enumerate(blocks):
            whole[i, :, j * LANES : (j + 1) * LANES] = whole_in[i, :, block]
        at = slice(i * width, (i + 1) * width)
        packed[:, at] = mm(picked, whole[i]).astype(BF)
        store(i, at)
    cut = mm(pick_rows(rest), whole[0, :, :half])
    cut += mm(pick_rows(rest, 4), whole[0, :, half:])
    cut += mm(pick_rows(rest, 2), whole[1, :, :half])
    cut += mm(pick_rows(rest, 6), whole[1, :, half:])
    packed[:, 2 * width : 2 * width + half] = cut.astype(BF)
    lane_ids = iota((LANES, tok_count), 0)
    gate_rows = jnp.zeros((rows, LANES), F32)
    for k in range(2):
        gate = gates[k : k + 1, :].astype(F32)
        first = jnp.where(lane_ids == 0, gate, 0.0).astype(BF)
        second = jnp.where(lane_ids == 1, gate, 0.0).astype(BF)
        gate_rows += mm(one_hot(main[k] == row_ids), first, NT)
        gate_rows += mm(one_hot(rest[k] == row_ids), second, NT)
    packed[:, 2 * width + half :] = gate_rows.astype(BF)
    store(2, slice(2 * width, packed.shape[1]))
    for copy in stores:
        copy.wait()


def stack_kernel(*refs):
    out = refs[-1]
    at = 0
    for ref in refs[:-1]:
        out[at : at + ref.shape[0]] = ref[...]
        at += ref.shape[0]


def stack(blocks):
    rows, columns = sum(b.shape[0] for b in blocks), blocks[0].shape[1]
    return call(
        stack_kernel,
        jax.ShapeDtypeStruct((rows, columns), BF),
        "stack",
        8,
        cost_estimate=pl.CostEstimate(flops=0, bytes_accessed=2 * rows * columns, transcendentals=0),
    )(*blocks)


def slot_kernel(got_in, w0, w1, w2, w3, mine, first, later, pre_out, gate_out, *scratch):
    x_all, dy_all, got, weights, sems = scratch
    rows = got.shape[0]
    hidden_width = w0.shape[1] // 3
    half = w0.shape[0] + w1.shape[0]
    width = 2 * half
    extra = rows // MAIN * 2
    source = iota((extra, rows), 0)
    base = source // 2 * MAIN + source % 2
    column = iota((extra, rows), 1)
    loads = []
    for at in (slice(2 * width, got.shape[1]), slice(0, width), slice(width, 2 * width)):
        loads.append((got_in.at[:, at], got.at[:, at]))
    at = 0
    for w in (w0, w1, w2, w3):
        loads.append((w, weights.at[at : at + w.shape[0]]))
        at += w.shape[0]
    loads = [pltpu.make_async_copy(a, b, sems.at[i]) for i, (a, b) in enumerate(loads)]
    for load in loads:
        load.start()
    loads[0].wait()
    cut = got[:, 2 * width : 2 * width + half]
    head = one_hot(column == base)
    x_all[rows:, :half] = mm(head, cut).astype(BF)
    x_all[rows:, half:] = mm(one_hot(column == base + 4), cut).astype(BF)
    loads[1].wait()
    x_all[:rows] = got[:, :width]
    loads[2].wait()
    dy_all[:rows] = got[:, width : 2 * width]
    dy_all[rows:, :half] = mm(one_hot(column == base + 2), cut).astype(BF)
    dy_all[rows:, half:] = mm(one_hot(column == base + 6), cut).astype(BF)
    gate_block = got[:, 2 * width + half :]
    gate = jnp.concatenate(
        [gate_block[:, 0:1].astype(F32), mm(head, gate_block)[:, 1:2]], axis=0
    )
    wide = slice(0, 2 * hidden_width)
    down = slice(2 * hidden_width, 3 * hidden_width)
    for load in loads[3:]:
        load.wait()
    pre = mm(x_all[...], weights[:, wide])
    upstream = mm(dy_all[...], weights[:, down])
    a = pre[:, :hidden_width]
    b = pre[:, hidden_width:]
    sig = jax.nn.sigmoid(a)
    silu = a * sig
    hidden32 = (silu * b).astype(BF).astype(F32)
    gate_grad = jnp.sum(upstream * hidden32, axis=1, keepdims=True)
    gate_out[...] = jnp.broadcast_to(gate_grad, gate_out.shape).astype(BF)
    hidden_grad = gate * upstream
    pre_out[:, :hidden_width] = (hidden_grad * b * sig * (1.0 + a * (1.0 - sig))).astype(BF)
    pre_out[:, hidden_width:] = (hidden_grad * silu).astype(BF)
    gated = (gate * hidden32).astype(BF)
    at = half
    for out in (first, later, mine):
        at = 0 if out is mine else at
        for d in range(0, out.shape[0], LANES):
            cols = slice(at, at + LANES)
            out[d : d + LANES, wide] = mm(x_all[:, cols], pre_out[...], TN).astype(BF)
            out[d : d + LANES, down] = mm(dy_all[:, cols], gated, TN).astype(BF)
            at += LANES


def back_kernel(pre_grad, gate_grad, w0, w1, w2, w3, back, cut_rows):
    total, columns = pre_grad.shape
    width = 2 * (w0.shape[0] + w1.shape[0])
    rows = back.shape[0]
    extra = total - rows
    quarter = width // 4
    at = 0
    for w in (w0, w1, w2, w3):
        grad = mm(pre_grad[...], w[:, :columns], NT).astype(BF)
        back[:, at : at + w.shape[0]] = grad[:rows]
        cut_rows[:, at : at + w.shape[0]] = grad[rows:]
        at += w.shape[0]
    row = iota((rows, extra), 0)
    column = iota((rows, extra), 1)
    target = row // MAIN * 2 + row % 2
    part = row % MAIN // 2
    cut = jnp.zeros((rows, quarter), F32)
    for h in range(4):
        cols = slice(h * quarter, (h + 1) * quarter)
        cut += mm(one_hot((column == target) & (part == h)), cut_rows[:, cols])
    back[:, width : width + quarter] = cut.astype(BF)
    lane = iota((rows, LANES), 1)
    spread = mm(one_hot((column == target) & (part == 0)), gate_grad[rows:])
    gate_rows = jnp.where(lane == 0, gate_grad[:rows].astype(F32), spread)
    back[:, width + quarter :] = jnp.where(lane < 2, gate_rows, 0.0).astype(BF)


def join_kernel(z, core, back, places, token_grad, gate_grad):
    tok_count, width = token_grad.shape
    rows = back.shape[0]
    quarter = width // 4
    row_ids = iota((rows, tok_count), 0)
    main = [places[k : k + 1, :] for k in range(2)]
    rest = [places[2 + k : 3 + k, :] for k in range(2)]
    whole = one_hot((main[0] == row_ids) | (main[1] == row_ids))
    cut = back[:, width : width + quarter]
    blocks = feature_blocks((z, core), width // (2 * LANES))
    for h in range(4):
        cols = slice(h * quarter, (h + 1) * quarter)
        here = one_hot((rest[0] + 2 * h == row_ids) | (rest[1] + 2 * h == row_ids))
        total = mm(whole, back[:, cols], TN) + mm(here, cut, TN)
        for j in range(quarter // LANES):
            block = blocks[h * (quarter // LANES) + j]
            token_grad[:, block] = total[:, j * LANES : (j + 1) * LANES].astype(BF)
    gate_rows = back[:, width + quarter :]
    for k in range(2):
        value = mm(gate_rows, one_hot(main[k] == row_ids), TN)[0:1, :]
        value += mm(gate_rows, one_hot(rest[k] == row_ids), TN)[1:2, :]
        gate_grad[k : k + 1, :] = value.astype(BF)


def expert_kernel(groups, plan, mixed, out):
    out[...] = jnp.zeros_like(out)
    for s in range(mixed.shape[0]):
        e = plan[s]
        out[e] += mixed[s].astype(F32)
    out[...] = out[...] * (1.0 / groups)


def move(array, step):
    chips = lax.axis_size("z")
    pairs = []
    for z in range(chips):
        pairs.append((2 * z, 2 * ((z + step) % chips)))
        pairs.append((2 * z + 1, 2 * ((z - step) % chips) + 1))
    return lax.ppermute(array, ("z", "core"), pairs)


def swap(array):
    return lax.ppermute(array, "core", [(0, 1), (1, 0)])


def local(tokens, out_grad, routes, gates, w_gate_up, w_down, plan, failed):
    chips = lax.axis_size("z")
    groups = chips * 2
    slots = lax.axis_size("ep")
    tok_count, width = tokens.shape
    hidden_width = w_down.shape[2]
    columns = 3 * hidden_width
    experts = slots // 2
    rows = slots * MAIN
    total = slots * (MAIN + 2)
    each = width // (groups * slots)
    smem = pl.BlockSpec(memory_space=pltpu.SMEM)
    vmem = pl.BlockSpec(memory_space=pltpu.VMEM)
    anywhere = pl.BlockSpec(memory_space=pl.ANY)
    place = [lax.axis_index(name).reshape(1) for name in ("z", "core")]

    sent, places = call(
        pack_kernel,
        (
            jax.ShapeDtypeStruct((rows, 2 * width + width // 2 + LANES), BF),
            jax.ShapeDtypeStruct((8, tok_count), jnp.int32),
        ),
        "pack",
        56,
        in_specs=[smem] * 2 + [vmem] * 4 + [anywhere] * 2,
        out_specs=(anywhere, vmem),
        scratch_shapes=[
            pltpu.VMEM((2, tok_count, width), BF),
            pltpu.VMEM((2, tok_count, width), BF),
            pltpu.VMEM((rows, 2 * width + width // 2 + LANES), BF),
            pltpu.SemaphoreType.DMA((2,)),
            pltpu.SemaphoreType.DMA((3,)),
        ],
    )(
        *place,
        routes.T,
        gates.T,
        plan.reshape(1, slots),
        failed,
        tokens,
        out_grad,
    )
    sent, w_gate_up, w_down = lax.optimization_barrier((sent, w_gate_up, w_down))
    got = lax.all_to_all(sent, "ep", split_axis=0, concat_axis=0, tiled=True)
    own = jnp.concatenate([w_gate_up[0], w_down[0]], axis=1)
    below, above = move(own, 1), move(own, -1)
    third, above2 = move(below, 2), move(above, -1)
    last, above3 = move(stack([third, below]), 1), move(above2, -1)
    w_mine = [stack([last, above3]), stack([third, above2, below, above, own])]
    w_all = w_mine + [swap(w) for w in w_mine]

    part = width // groups
    mine, first, later, pre_grad, gate_rows = call(
        slot_kernel,
        (
            jax.ShapeDtypeStruct((width // 2, columns), BF),
            jax.ShapeDtypeStruct((FIRST * part, columns), BF),
            jax.ShapeDtypeStruct((width // 2 - FIRST * part, columns), BF),
            jax.ShapeDtypeStruct((total, 2 * hidden_width), BF),
            jax.ShapeDtypeStruct((total, LANES), BF),
        ),
        "slot",
        32,
        in_specs=[anywhere] * 5,
        scratch_shapes=[
            pltpu.VMEM((total, width), BF),
            pltpu.VMEM((total, width), BF),
            pltpu.VMEM(sent.shape, BF),
            pltpu.VMEM((width, columns), BF),
            pltpu.SemaphoreType.DMA((7,)),
        ],
    )(got, *w_all)
    first, later = swap(first), swap(later)

    def both(j, n=1):
        theirs, at = (first, j) if j < FIRST else (later, j - FIRST)
        return (
            mine[j * part : (j + n) * part].astype(F32)
            + theirs[at * part : (at + n) * part].astype(F32)
        )

    minus, plus = both(0, 2).astype(BF), both(2).astype(BF)
    minus, plus, pre_grad = lax.optimization_barrier((minus, plus, pre_grad))
    back = call(
        back_kernel,
        jax.ShapeDtypeStruct((rows, width + width // 4 + LANES), BF),
        "back",
        24,
        in_specs=[vmem] * 6,
        scratch_shapes=[pltpu.VMEM((total - rows, width), BF)],
    )(pre_grad, gate_rows, *w_all)
    minus, plus = move(minus, -1), move(plus, 1)
    far_sum = (minus[:part].astype(F32) + both(3)).astype(BF)
    plus = (plus.astype(F32) + both(4)).astype(BF)
    far_sum, plus = move(far_sum, -2), move(plus, 1)
    minus = (far_sum.astype(F32) + minus[part:].astype(F32) + both(5)).astype(BF)
    plus = (plus.astype(F32) + both(6)).astype(BF)
    minus, plus = move(minus, -1), move(plus, 1)
    owned = (minus.astype(F32) + plus.astype(F32) + both(7)).astype(BF)

    back = lax.all_to_all(back, "ep", split_axis=0, concat_axis=0, tiled=True)
    owned, back = lax.optimization_barrier((owned, back))
    token_grad, gate_grad = call(
        join_kernel,
        (
            jax.ShapeDtypeStruct((tok_count, width), BF),
            jax.ShapeDtypeStruct((2, tok_count), BF),
        ),
        "join",
        16,
        in_specs=[smem, smem, vmem, vmem],
    )(*place, back, places)
    owned = owned.reshape(slots, each, columns)
    mixed = lax.all_to_all(owned, "ep", split_axis=0, concat_axis=0, tiled=True)
    weight_grad = call(
        functools.partial(expert_kernel, groups),
        jax.ShapeDtypeStruct((experts, each, columns), F32),
        "experts",
        8,
        in_specs=[smem, vmem],
    )(plan, mixed)
    return token_grad, gate_grad.T, weight_grad


def solution(mesh):
    devices = mesh.devices.reshape(mesh.shape["grp"] // 2, 2, mesh.shape["ep"])
    fine = jax.sharding.Mesh(devices, ("z", "core", "ep"))
    everywhere = P(("z", "core", "ep"), None)
    weight = P("ep", ("z", "core"), None)
    return jax.shard_map(
        local,
        mesh=fine,
        in_specs=(everywhere,) * 4 + (weight, weight, P(), P()),
        out_specs=(everywhere, everywhere, P(None, ("z", "core", "ep"), None)),
        check_vma=False,
    )
```

```python
import functools

import jax
import jax.numpy as jnp
from jax import lax
from jax.experimental import pallas as pl
from jax.experimental.pallas import tpu as pltpu
from jax.sharding import PartitionSpec as P

BF = jnp.bfloat16
F32 = jnp.float32
LANES = 128
MAIN = 8
TN = (((0,), (0,)), ((), ()))
NT = (((1,), (1,)), ((), ()))


def mm(a, b, dims=(((1,), (0,)), ((), ()))):
    return lax.dot_general(a, b, dims, preferred_element_type=F32)


def iota(shape, dim):
    return lax.broadcasted_iota(jnp.int32, shape, dim)


def one_hot(cond):
    return jnp.where(cond, 1.0, 0.0).astype(BF)


def call(kernel, outs, name, mib, **kw):
    return pl.pallas_call(
        kernel,
        out_shape=outs,
        name=name,
        compiler_params=pltpu.CompilerParams(vmem_limit_bytes=mib * 2**20),
        **kw,
    )


ORDER = (-4, -2, 3, -3, 2, -1, 1, 0)
FIRST = 3


def feature_blocks(place, chips):
    blocks = []
    z, mine = place[0][0], place[1][0]
    for core in (mine, 1 - mine):
        for shift in ORDER:
            chip = lax.rem(z + (1 - 2 * core) * shift + chips, chips)
            blocks.append(pl.ds(pl.multiple_of((2 * chip + core) * LANES, LANES), LANES))
    return blocks


def pack_kernel(
    z, core, routes, gates, plan, failed, tokens_in, grads_in, sent, places, *scratch
):
    whole_in, whole, packed, in_sems, out_sems = scratch
    tok_count, width = tokens_in.shape
    slots = plan.shape[1]
    half = width // 2
    rows = slots * MAIN
    loads = []
    for i, ref in enumerate((tokens_in, grads_in)):
        loads.append(pltpu.make_async_copy(ref, whole_in.at[i], in_sems.at[i]))
        loads[i].start()
    in_group = iota(failed.shape, 0) == 2 * z[0] + core[0]
    dead = jnp.sum(jnp.where(in_group, failed[...], 0), axis=0, keepdims=True)
    hosting = jnp.where(dead == 0, plan[...], -1)
    diagonal = iota((slots, slots), 0) == iota((slots, slots), 1)
    hosting = jnp.sum(jnp.where(diagonal, hosting, 0), axis=1, keepdims=True)
    slot_ids = iota((slots, tok_count), 0).astype(F32)
    before_slot = one_hot(iota((slots, slots), 1) < iota((slots, slots), 0))
    before_tok = one_hot(iota((tok_count, tok_count), 0) < iota((tok_count, tok_count), 1))
    experts = iota((slots, tok_count), 0)
    ids = [routes[k : k + 1, :] for k in range(2)]
    hot = [jnp.where(experts == i, 1.0, 0.0) for i in ids]
    prefix = mm((hot[0] + hot[1]).astype(BF), before_tok)
    rank = [
        jnp.sum(hot[0] * prefix, axis=0, keepdims=True),
        jnp.sum(hot[1] * (prefix + hot[0]), axis=0, keepdims=True),
    ]
    chosen = []
    for k in range(2):
        cand = jnp.where(hosting == ids[k], 1.0, 0.0)
        ordinal = mm(before_slot, cand.astype(BF))
        count = jnp.maximum(jnp.sum(cand, axis=0, keepdims=True), 1.0)
        pick = rank[k] - count * jnp.floor((rank[k] + 0.5) / count)
        chosen.append(jnp.where(ordinal == pick, cand, 0.0))
    prefix = mm((chosen[0] + chosen[1]).astype(BF), before_tok)
    position = [
        jnp.sum(chosen[0] * prefix, axis=0, keepdims=True),
        jnp.sum(chosen[1] * (prefix + chosen[0]), axis=0, keepdims=True),
    ]
    row_ids = iota((rows, tok_count), 0)
    main, rest = [], []
    for k in range(2):
        slot = jnp.sum(chosen[k] * slot_ids, axis=0, keepdims=True).astype(jnp.int32)
        pos = position[k].astype(jnp.int32)
        main.append(jnp.where(pos < MAIN, slot * MAIN + pos, -64))
        rest.append(jnp.where(pos < MAIN, -64, slot * MAIN + pos - MAIN))
    line = iota(places.shape, 0)
    noted = jnp.full(places.shape, -64, jnp.int32)
    for i, at in enumerate(main + rest):
        noted = jnp.where(line == i, at, noted)
    places[...] = noted

    def pick_rows(at, shift=0):
        return one_hot((at[0] + shift == row_ids) | (at[1] + shift == row_ids))

    stores = []

    def store(i, at):
        stores.append(pltpu.make_async_copy(packed.at[:, at], sent.at[:, at], out_sems.at[i]))
        stores[i].start()

    blocks = feature_blocks((z, core), width // (2 * LANES))
    picked = pick_rows(main)
    for i in range(2):
        loads[i].wait()
        for j, block in enumerate(blocks):
            whole[i, :, j * LANES : (j + 1) * LANES] = whole_in[i, :, block]
        at = slice(i * width, (i + 1) * width)
        packed[:, at] = mm(picked, whole[i]).astype(BF)
        store(i, at)
    cut = mm(pick_rows(rest), whole[0, :, :half])
    cut += mm(pick_rows(rest, 4), whole[0, :, half:])
    cut += mm(pick_rows(rest, 2), whole[1, :, :half])
    cut += mm(pick_rows(rest, 6), whole[1, :, half:])
    packed[:, 2 * width : 2 * width + half] = cut.astype(BF)
    lane_ids = iota((LANES, tok_count), 0)
    gate_rows = jnp.zeros((rows, LANES), F32)
    for k in range(2):
        gate = gates[k : k + 1, :].astype(F32)
        first = jnp.where(lane_ids == 0, gate, 0.0).astype(BF)
        second = jnp.where(lane_ids == 1, gate, 0.0).astype(BF)
        gate_rows += mm(one_hot(main[k] == row_ids), first, NT)
        gate_rows += mm(one_hot(rest[k] == row_ids), second, NT)
    packed[:, 2 * width + half :] = gate_rows.astype(BF)
    store(2, slice(2 * width, packed.shape[1]))
    for copy in stores:
        copy.wait()


def stack_kernel(*refs):
    out = refs[-1]
    at = 0
    for ref in refs[:-1]:
        out[at : at + ref.shape[0]] = ref[...]
        at += ref.shape[0]


def stack(blocks):
    rows, columns = sum(b.shape[0] for b in blocks), blocks[0].shape[1]
    return call(
        stack_kernel,
        jax.ShapeDtypeStruct((rows, columns), BF),
        "stack",
        8,
        cost_estimate=pl.CostEstimate(flops=0, bytes_accessed=2 * rows * columns, transcendentals=0),
    )(*blocks)


def slot_kernel(got, weights, mine, first, later, pre_out, gate_out, x_all, dy_all):
    rows = got.shape[0]
    hidden_width = weights.shape[1] // 3
    width = weights.shape[0]
    half = width // 2
    extra = rows // MAIN * 2
    source = iota((extra, rows), 0)
    base = source // 2 * MAIN + source % 2
    column = iota((extra, rows), 1)
    cut = got[:, 2 * width : 2 * width + half]
    head = one_hot(column == base)
    x_all[rows:, :half] = mm(head, cut).astype(BF)
    x_all[rows:, half:] = mm(one_hot(column == base + 4), cut).astype(BF)
    x_all[:rows] = got[:, :width]
    dy_all[:rows] = got[:, width : 2 * width]
    dy_all[rows:, :half] = mm(one_hot(column == base + 2), cut).astype(BF)
    dy_all[rows:, half:] = mm(one_hot(column == base + 6), cut).astype(BF)
    gate_block = got[:, 2 * width + half :]
    gate = jnp.concatenate(
        [gate_block[:, 0:1].astype(F32), mm(head, gate_block)[:, 1:2]], axis=0
    )
    wide = slice(0, 2 * hidden_width)
    down = slice(2 * hidden_width, 3 * hidden_width)
    pre = mm(x_all[...], weights[:, wide])
    upstream = mm(dy_all[...], weights[:, down])
    a = pre[:, :hidden_width]
    b = pre[:, hidden_width:]
    sig = jax.nn.sigmoid(a)
    silu = a * sig
    hidden32 = (silu * b).astype(BF).astype(F32)
    gate_grad = jnp.sum(upstream * hidden32, axis=1, keepdims=True)
    gate_out[...] = jnp.broadcast_to(gate_grad, gate_out.shape).astype(BF)
    hidden_grad = gate * upstream
    pre_out[:, :hidden_width] = (hidden_grad * b * sig * (1.0 + a * (1.0 - sig))).astype(BF)
    pre_out[:, hidden_width:] = (hidden_grad * silu).astype(BF)
    gated = (gate * hidden32).astype(BF)
    at = half
    for out in (first, later, mine):
        at = 0 if out is mine else at
        for d in range(0, out.shape[0], LANES):
            cols = slice(at, at + LANES)
            out[d : d + LANES, wide] = mm(x_all[:, cols], pre_out[...], TN).astype(BF)
            out[d : d + LANES, down] = mm(dy_all[:, cols], gated, TN).astype(BF)
            at += LANES


def back_kernel(pre_grad, gate_grad, weights, back):
    total, columns = pre_grad.shape
    width = weights.shape[0]
    rows = back.shape[0]
    extra = total - rows
    quarter = width // 4
    row = iota((rows, extra), 0)
    column = iota((rows, extra), 1)
    target = row // MAIN * 2 + row % 2
    part = row % MAIN // 2
    cut = jnp.zeros((rows, quarter), F32)
    for h in range(4):
        cols = slice(h * quarter, (h + 1) * quarter)
        grad = mm(pre_grad[...], weights[cols, :columns], NT).astype(BF)
        back[:, cols] = grad[:rows]
        cut += mm(one_hot((column == target) & (part == h)), grad[rows:])
    back[:, width : width + quarter] = cut.astype(BF)
    lane = iota((rows, LANES), 1)
    spread = mm(one_hot((column == target) & (part == 0)), gate_grad[rows:])
    gate_rows = jnp.where(lane == 0, gate_grad[:rows].astype(F32), spread)
    back[:, width + quarter :] = jnp.where(lane < 2, gate_rows, 0.0).astype(BF)


def join_kernel(z, core, back, places, token_grad, gate_grad):
    tok_count, width = token_grad.shape
    rows = back.shape[0]
    quarter = width // 4
    row_ids = iota((rows, tok_count), 0)
    main = [places[k : k + 1, :] for k in range(2)]
    rest = [places[2 + k : 3 + k, :] for k in range(2)]
    whole = one_hot((main[0] == row_ids) | (main[1] == row_ids))
    cut = back[:, width : width + quarter]
    blocks = feature_blocks((z, core), width // (2 * LANES))
    for h in range(4):
        cols = slice(h * quarter, (h + 1) * quarter)
        here = one_hot((rest[0] + 2 * h == row_ids) | (rest[1] + 2 * h == row_ids))
        total = mm(whole, back[:, cols], TN) + mm(here, cut, TN)
        for j in range(quarter // LANES):
            block = blocks[h * (quarter // LANES) + j]
            token_grad[:, block] = total[:, j * LANES : (j + 1) * LANES].astype(BF)
    gate_rows = back[:, width + quarter :]
    for k in range(2):
        value = mm(gate_rows, one_hot(main[k] == row_ids), TN)[0:1, :]
        value += mm(gate_rows, one_hot(rest[k] == row_ids), TN)[1:2, :]
        gate_grad[k : k + 1, :] = value.astype(BF)


def expert_kernel(groups, plan, mixed, out):
    out[...] = jnp.zeros_like(out)
    for s in range(mixed.shape[0]):
        e = plan[s]
        out[e] += mixed[s].astype(F32)
    out[...] = out[...] * (1.0 / groups)


def move(array, step):
    chips = lax.axis_size("z")
    pairs = []
    for z in range(chips):
        pairs.append((2 * z, 2 * ((z + step) % chips)))
        pairs.append((2 * z + 1, 2 * ((z - step) % chips) + 1))
    return lax.ppermute(array, ("z", "core"), pairs)


def swap(array):
    return lax.ppermute(array, "core", [(0, 1), (1, 0)])


def local(tokens, out_grad, routes, gates, w_gate_up, w_down, plan, failed):
    chips = lax.axis_size("z")
    groups = chips * 2
    slots = lax.axis_size("ep")
    tok_count, width = tokens.shape
    hidden_width = w_down.shape[2]
    columns = 3 * hidden_width
    experts = slots // 2
    rows = slots * MAIN
    total = slots * (MAIN + 2)
    each = width // (groups * slots)
    smem = pl.BlockSpec(memory_space=pltpu.SMEM)
    vmem = pl.BlockSpec(memory_space=pltpu.VMEM)
    anywhere = pl.BlockSpec(memory_space=pl.ANY)
    place = [lax.axis_index(name).reshape(1) for name in ("z", "core")]

    sent, places = call(
        pack_kernel,
        (
            jax.ShapeDtypeStruct((rows, 2 * width + width // 2 + LANES), BF),
            jax.ShapeDtypeStruct((8, tok_count), jnp.int32),
        ),
        "pack",
        56,
        in_specs=[smem] * 2 + [vmem] * 4 + [anywhere] * 2,
        out_specs=(anywhere, vmem),
        scratch_shapes=[
            pltpu.VMEM((2, tok_count, width), BF),
            pltpu.VMEM((2, tok_count, width), BF),
            pltpu.VMEM((rows, 2 * width + width // 2 + LANES), BF),
            pltpu.SemaphoreType.DMA((2,)),
            pltpu.SemaphoreType.DMA((3,)),
        ],
    )(
        *place,
        routes.T,
        gates.T,
        plan.reshape(1, slots),
        failed,
        tokens,
        out_grad,
    )
    sent, w_gate_up, w_down = lax.optimization_barrier((sent, w_gate_up, w_down))
    got = lax.all_to_all(sent, "ep", split_axis=0, concat_axis=0, tiled=True)
    own = jnp.concatenate([w_gate_up[0], w_down[0]], axis=1)
    below, above = move(own, 1), move(own, -1)
    third, above2 = move(below, 2), move(above, -1)
    last, above3 = move(stack([third, below]), 1), move(above2, -1)
    w_mine = [stack([last, above3]), stack([third, above2, below, above, own])]
    w_all = stack(w_mine + [swap(w) for w in w_mine])

    part = width // groups
    mine, first, later, pre_grad, gate_rows = call(
        slot_kernel,
        (
            jax.ShapeDtypeStruct((width // 2, columns), BF),
            jax.ShapeDtypeStruct((FIRST * part, columns), BF),
            jax.ShapeDtypeStruct((width // 2 - FIRST * part, columns), BF),
            jax.ShapeDtypeStruct((total, 2 * hidden_width), BF),
            jax.ShapeDtypeStruct((total, LANES), BF),
        ),
        "slot",
        28,
        in_specs=[vmem] * 2,
        scratch_shapes=[
            pltpu.VMEM((total, width), BF),
            pltpu.VMEM((total, width), BF),
        ],
    )(got, w_all)
    first, later = swap(first), swap(later)

    def both(j, n=1):
        theirs, at = (first, j) if j < FIRST else (later, j - FIRST)
        return (
            mine[j * part : (j + n) * part].astype(F32)
            + theirs[at * part : (at + n) * part].astype(F32)
        )

    minus, plus = both(0, 2).astype(BF), both(2).astype(BF)
    minus, plus, pre_grad = lax.optimization_barrier((minus, plus, pre_grad))
    back = call(
        back_kernel,
        jax.ShapeDtypeStruct((rows, width + width // 4 + LANES), BF),
        "back",
        24,
        in_specs=[vmem] * 3,
    )(pre_grad, gate_rows, w_all)
    minus, plus = move(minus, -1), move(plus, 1)
    far_sum = (minus[:part].astype(F32) + both(3)).astype(BF)
    plus = (plus.astype(F32) + both(4)).astype(BF)
    far_sum, plus = move(far_sum, -2), move(plus, 1)
    minus = (far_sum.astype(F32) + minus[part:].astype(F32) + both(5)).astype(BF)
    plus = (plus.astype(F32) + both(6)).astype(BF)
    minus, plus = move(minus, -1), move(plus, 1)
    owned = (minus.astype(F32) + plus.astype(F32) + both(7)).astype(BF)

    back = lax.all_to_all(back, "ep", split_axis=0, concat_axis=0, tiled=True)
    owned, back = lax.optimization_barrier((owned, back))
    token_grad, gate_grad = call(
        join_kernel,
        (
            jax.ShapeDtypeStruct((tok_count, width), BF),
            jax.ShapeDtypeStruct((2, tok_count), BF),
        ),
        "join",
        16,
        in_specs=[smem, smem, vmem, vmem],
    )(*place, back, places)
    owned = owned.reshape(slots, each, columns)
    mixed = lax.all_to_all(owned, "ep", split_axis=0, concat_axis=0, tiled=True)
    weight_grad = call(
        functools.partial(expert_kernel, groups),
        jax.ShapeDtypeStruct((experts, each, columns), F32),
        "experts",
        8,
        in_specs=[smem, vmem],
    )(plan, mixed)
    return token_grad, gate_grad.T, weight_grad


def solution(mesh):
    devices = mesh.devices.reshape(mesh.shape["grp"] // 2, 2, mesh.shape["ep"])
    fine = jax.sharding.Mesh(devices, ("z", "core", "ep"))
    everywhere = P(("z", "core", "ep"), None)
    weight = P("ep", ("z", "core"), None)
    return jax.shard_map(
        local,
        mesh=fine,
        in_specs=(everywhere,) * 4 + (weight, weight, P(), P()),
        out_specs=(everywhere, everywhere, P(None, ("z", "core", "ep"), None)),
        check_vma=False,
    )
```

```python
import functools

import jax
import jax.numpy as jnp
from jax import lax
from jax.experimental import pallas as pl
from jax.experimental.pallas import tpu as pltpu
from jax.sharding import PartitionSpec as P

BF = jnp.bfloat16
F32 = jnp.float32
LANES = 128
MAIN = 8
TN = (((0,), (0,)), ((), ()))
NT = (((1,), (1,)), ((), ()))


def mm(a, b, dims=(((1,), (0,)), ((), ()))):
    return lax.dot_general(a, b, dims, preferred_element_type=F32)


def iota(shape, dim):
    return lax.broadcasted_iota(jnp.int32, shape, dim)


def one_hot(cond):
    return jnp.where(cond, 1.0, 0.0).astype(BF)


def call(kernel, outs, name, mib, **kw):
    return pl.pallas_call(
        kernel,
        out_shape=outs,
        name=name,
        compiler_params=pltpu.CompilerParams(vmem_limit_bytes=mib * 2**20),
        **kw,
    )


ORDER = (-4, -2, 3, -3, 2, -1, 1, 0)
FIRST = 3


def feature_blocks(place, chips):
    blocks = []
    z, mine = place[0][0], place[1][0]
    for core in (mine, 1 - mine):
        for shift in ORDER:
            chip = lax.rem(z + (1 - 2 * core) * shift + chips, chips)
            blocks.append(pl.ds(pl.multiple_of((2 * chip + core) * LANES, LANES), LANES))
    return blocks


def pack_kernel(
    z, core, routes, gates, plan, failed, tokens_in, grads_in, sent, places, *scratch
):
    whole_in, whole, packed, in_sems, out_sems = scratch
    tok_count, width = tokens_in.shape
    slots = plan.shape[1]
    half = width // 2
    rows = slots * MAIN
    loads = []
    for i, ref in enumerate((tokens_in, grads_in)):
        loads.append(pltpu.make_async_copy(ref, whole_in.at[i], in_sems.at[i]))
        loads[i].start()
    in_group = iota(failed.shape, 0) == 2 * z[0] + core[0]
    dead = jnp.sum(jnp.where(in_group, failed[...], 0), axis=0, keepdims=True)
    hosting = jnp.where(dead == 0, plan[...], -1)
    diagonal = iota((slots, slots), 0) == iota((slots, slots), 1)
    hosting = jnp.sum(jnp.where(diagonal, hosting, 0), axis=1, keepdims=True)
    slot_ids = iota((slots, tok_count), 0).astype(F32)
    before_slot = one_hot(iota((slots, slots), 1) < iota((slots, slots), 0))
    before_tok = one_hot(iota((tok_count, tok_count), 0) < iota((tok_count, tok_count), 1))
    experts = iota((slots, tok_count), 0)
    ids = [routes[k : k + 1, :] for k in range(2)]
    hot = [jnp.where(experts == i, 1.0, 0.0) for i in ids]
    prefix = mm((hot[0] + hot[1]).astype(BF), before_tok)
    rank = [
        jnp.sum(hot[0] * prefix, axis=0, keepdims=True),
        jnp.sum(hot[1] * (prefix + hot[0]), axis=0, keepdims=True),
    ]
    chosen = []
    for k in range(2):
        cand = jnp.where(hosting == ids[k], 1.0, 0.0)
        ordinal = mm(before_slot, cand.astype(BF))
        count = jnp.maximum(jnp.sum(cand, axis=0, keepdims=True), 1.0)
        pick = rank[k] - count * jnp.floor((rank[k] + 0.5) / count)
        chosen.append(jnp.where(ordinal == pick, cand, 0.0))
    prefix = mm((chosen[0] + chosen[1]).astype(BF), before_tok)
    position = [
        jnp.sum(chosen[0] * prefix, axis=0, keepdims=True),
        jnp.sum(chosen[1] * (prefix + chosen[0]), axis=0, keepdims=True),
    ]
    row_ids = iota((rows, tok_count), 0)
    main, rest = [], []
    for k in range(2):
        slot = jnp.sum(chosen[k] * slot_ids, axis=0, keepdims=True).astype(jnp.int32)
        pos = position[k].astype(jnp.int32)
        main.append(jnp.where(pos < MAIN, slot * MAIN + pos, -64))
        rest.append(jnp.where(pos < MAIN, -64, slot * MAIN + pos - MAIN))
    line = iota(places.shape, 0)
    noted = jnp.full(places.shape, -64, jnp.int32)
    for i, at in enumerate(main + rest):
        noted = jnp.where(line == i, at, noted)
    places[...] = noted

    def pick_rows(at, shift=0):
        return one_hot((at[0] + shift == row_ids) | (at[1] + shift == row_ids))

    stores = []

    def store(i, at):
        stores.append(pltpu.make_async_copy(packed.at[:, at], sent.at[:, at], out_sems.at[i]))
        stores[i].start()

    blocks = feature_blocks((z, core), width // (2 * LANES))
    picked = pick_rows(main)
    for i in range(2):
        loads[i].wait()
        for j, block in enumerate(blocks):
            whole[i, :, j * LANES : (j + 1) * LANES] = whole_in[i, :, block]
        at = slice(i * width, (i + 1) * width)
        packed[:, at] = mm(picked, whole[i]).astype(BF)
        store(i, at)
    cut = mm(pick_rows(rest), whole[0, :, :half])
    cut += mm(pick_rows(rest, 4), whole[0, :, half:])
    cut += mm(pick_rows(rest, 2), whole[1, :, :half])
    cut += mm(pick_rows(rest, 6), whole[1, :, half:])
    packed[:, 2 * width : 2 * width + half] = cut.astype(BF)
    lane_ids = iota((LANES, tok_count), 0)
    gate_rows = jnp.zeros((rows, LANES), F32)
    for k in range(2):
        gate = gates[k : k + 1, :].astype(F32)
        first = jnp.where(lane_ids == 0, gate, 0.0).astype(BF)
        second = jnp.where(lane_ids == 1, gate, 0.0).astype(BF)
        gate_rows += mm(one_hot(main[k] == row_ids), first, NT)
        gate_rows += mm(one_hot(rest[k] == row_ids), second, NT)
    packed[:, 2 * width + half :] = gate_rows.astype(BF)
    store(2, slice(2 * width, packed.shape[1]))
    for copy in stores:
        copy.wait()


def stack_kernel(*refs):
    out = refs[-1]
    at = 0
    for ref in refs[:-1]:
        out[at : at + ref.shape[0]] = ref[...]
        at += ref.shape[0]


def stack(blocks):
    rows, columns = sum(b.shape[0] for b in blocks), blocks[0].shape[1]
    return call(
        stack_kernel,
        jax.ShapeDtypeStruct((rows, columns), BF),
        "stack",
        8,
        cost_estimate=pl.CostEstimate(flops=0, bytes_accessed=2 * rows * columns, transcendentals=0),
    )(*blocks)


def slot_kernel(got_in, w0, w1, w2, w3, mine, first, later, pre_out, gate_out, *scratch):
    x_all, dy_all, got, weights, sems = scratch
    rows = got.shape[0]
    hidden_width = w0.shape[1] // 3
    half = w0.shape[0] + w1.shape[0]
    width = 2 * half
    extra = rows // MAIN * 2
    source = iota((extra, rows), 0)
    base = source // 2 * MAIN + source % 2
    column = iota((extra, rows), 1)
    loads = []
    for at in (slice(2 * width, got.shape[1]), slice(0, width), slice(width, 2 * width)):
        loads.append((got_in.at[:, at], got.at[:, at]))
    at = 0
    for w in (w0, w1, w2, w3):
        loads.append((w, weights.at[at : at + w.shape[0]]))
        at += w.shape[0]
    loads = [pltpu.make_async_copy(a, b, sems.at[i]) for i, (a, b) in enumerate(loads)]
    for load in loads:
        load.start()
    loads[0].wait()
    cut = got[:, 2 * width : 2 * width + half]
    head = one_hot(column == base)
    x_all[rows:, :half] = mm(head, cut).astype(BF)
    x_all[rows:, half:] = mm(one_hot(column == base + 4), cut).astype(BF)
    loads[1].wait()
    x_all[:rows] = got[:, :width]
    loads[2].wait()
    dy_all[:rows] = got[:, width : 2 * width]
    dy_all[rows:, :half] = mm(one_hot(column == base + 2), cut).astype(BF)
    dy_all[rows:, half:] = mm(one_hot(column == base + 6), cut).astype(BF)
    gate_block = got[:, 2 * width + half :]
    gate = jnp.concatenate(
        [gate_block[:, 0:1].astype(F32), mm(head, gate_block)[:, 1:2]], axis=0
    )
    wide = slice(0, 2 * hidden_width)
    down = slice(2 * hidden_width, 3 * hidden_width)
    for load in loads[3:]:
        load.wait()
    pre = mm(x_all[...], weights[:, wide])
    upstream = mm(dy_all[...], weights[:, down])
    a = pre[:, :hidden_width]
    b = pre[:, hidden_width:]
    sig = jax.nn.sigmoid(a)
    silu = a * sig
    hidden32 = (silu * b).astype(BF).astype(F32)
    gate_grad = jnp.sum(upstream * hidden32, axis=1, keepdims=True)
    gate_out[...] = jnp.broadcast_to(gate_grad, gate_out.shape).astype(BF)
    hidden_grad = gate * upstream
    pre_out[:, :hidden_width] = (hidden_grad * b * sig * (1.0 + a * (1.0 - sig))).astype(BF)
    pre_out[:, hidden_width:] = (hidden_grad * silu).astype(BF)
    gated = (gate * hidden32).astype(BF)
    at = half
    for out in (first, later, mine):
        at = 0 if out is mine else at
        for d in range(0, out.shape[0], LANES):
            cols = slice(at, at + LANES)
            out[d : d + LANES, wide] = mm(x_all[:, cols], pre_out[...], TN).astype(BF)
            out[d : d + LANES, down] = mm(dy_all[:, cols], gated, TN).astype(BF)
            at += LANES


def back_kernel(pre_grad, gate_grad, w0, w1, w2, w3, back, cut_rows):
    total, columns = pre_grad.shape
    width = 2 * (w0.shape[0] + w1.shape[0])
    rows = back.shape[0]
    extra = total - rows
    quarter = width // 4
    at = 0
    for w in (w0, w1, w2, w3):
        grad = mm(pre_grad[...], w[:, :columns], NT).astype(BF)
        back[:, at : at + w.shape[0]] = grad[:rows]
        cut_rows[:, at : at + w.shape[0]] = grad[rows:]
        at += w.shape[0]
    row = iota((rows, extra), 0)
    column = iota((rows, extra), 1)
    target = row // MAIN * 2 + row % 2
    part = row % MAIN // 2
    cut = jnp.zeros((rows, quarter), F32)
    for h in range(4):
        cols = slice(h * quarter, (h + 1) * quarter)
        cut += mm(one_hot((column == target) & (part == h)), cut_rows[:, cols])
    back[:, width : width + quarter] = cut.astype(BF)
    lane = iota((rows, LANES), 1)
    spread = mm(one_hot((column == target) & (part == 0)), gate_grad[rows:])
    gate_rows = jnp.where(lane == 0, gate_grad[:rows].astype(F32), spread)
    back[:, width + quarter :] = jnp.where(lane < 2, gate_rows, 0.0).astype(BF)


def join_kernel(z, core, back, places, token_grad, gate_grad):
    tok_count, width = token_grad.shape
    rows = back.shape[0]
    quarter = width // 4
    row_ids = iota((rows, tok_count), 0)
    main = [places[k : k + 1, :] for k in range(2)]
    rest = [places[2 + k : 3 + k, :] for k in range(2)]
    whole = one_hot((main[0] == row_ids) | (main[1] == row_ids))
    cut = back[:, width : width + quarter]
    blocks = feature_blocks((z, core), width // (2 * LANES))
    for h in range(4):
        cols = slice(h * quarter, (h + 1) * quarter)
        here = one_hot((rest[0] + 2 * h == row_ids) | (rest[1] + 2 * h == row_ids))
        total = mm(whole, back[:, cols], TN) + mm(here, cut, TN)
        for j in range(quarter // LANES):
            block = blocks[h * (quarter // LANES) + j]
            token_grad[:, block] = total[:, j * LANES : (j + 1) * LANES].astype(BF)
    gate_rows = back[:, width + quarter :]
    for k in range(2):
        value = mm(gate_rows, one_hot(main[k] == row_ids), TN)[0:1, :]
        value += mm(gate_rows, one_hot(rest[k] == row_ids), TN)[1:2, :]
        gate_grad[k : k + 1, :] = value.astype(BF)


def expert_kernel(groups, plan, mixed, out):
    out[...] = jnp.zeros_like(out)
    for s in range(mixed.shape[0]):
        e = plan[s]
        out[e] += mixed[s].astype(F32)
    out[...] = out[...] * (1.0 / groups)


def move(array, step):
    chips = lax.axis_size("z")
    pairs = []
    for z in range(chips):
        pairs.append((2 * z, 2 * ((z + step) % chips)))
        pairs.append((2 * z + 1, 2 * ((z - step) % chips) + 1))
    return lax.ppermute(array, ("z", "core"), pairs)


def swap(array):
    return lax.ppermute(array, "core", [(0, 1), (1, 0)])


def local(tokens, out_grad, routes, gates, w_gate_up, w_down, plan, failed):
    chips = lax.axis_size("z")
    groups = chips * 2
    slots = lax.axis_size("ep")
    tok_count, width = tokens.shape
    hidden_width = w_down.shape[2]
    columns = 3 * hidden_width
    experts = slots // 2
    rows = slots * MAIN
    total = slots * (MAIN + 2)
    each = width // (groups * slots)
    smem = pl.BlockSpec(memory_space=pltpu.SMEM)
    vmem = pl.BlockSpec(memory_space=pltpu.VMEM)
    anywhere = pl.BlockSpec(memory_space=pl.ANY)
    place = [lax.axis_index(name).reshape(1) for name in ("z", "core")]

    sent, places = call(
        pack_kernel,
        (
            jax.ShapeDtypeStruct((rows, 2 * width + width // 2 + LANES), BF),
            jax.ShapeDtypeStruct((8, tok_count), jnp.int32),
        ),
        "pack",
        56,
        in_specs=[smem] * 2 + [vmem] * 4 + [anywhere] * 2,
        out_specs=(anywhere, vmem),
        scratch_shapes=[
            pltpu.VMEM((2, tok_count, width), BF),
            pltpu.VMEM((2, tok_count, width), BF),
            pltpu.VMEM((rows, 2 * width + width // 2 + LANES), BF),
            pltpu.SemaphoreType.DMA((2,)),
            pltpu.SemaphoreType.DMA((3,)),
        ],
    )(
        *place,
        routes.T,
        gates.T,
        plan.reshape(1, slots),
        failed,
        tokens,
        out_grad,
    )
    sent, w_gate_up, w_down = lax.optimization_barrier((sent, w_gate_up, w_down))
    got = lax.all_to_all(sent, "ep", split_axis=0, concat_axis=0, tiled=True)
    own = jnp.concatenate([w_gate_up[0], w_down[0]], axis=1)
    below, above = move(own, 1), move(own, -1)
    third, above2 = move(below, 2), move(above, -1)
    last, above3 = move(stack([third, below]), 1), move(above2, -1)
    w_mine = [stack([last, above3]), stack([third, above2, below, above, own])]
    w_all = w_mine + [swap(w) for w in w_mine]

    part = width // groups
    mine, first, later, pre_grad, gate_rows = call(
        slot_kernel,
        (
            jax.ShapeDtypeStruct((width // 2, columns), BF),
            jax.ShapeDtypeStruct((FIRST * part, columns), BF),
            jax.ShapeDtypeStruct((width // 2 - FIRST * part, columns), BF),
            jax.ShapeDtypeStruct((total, 2 * hidden_width), BF),
            jax.ShapeDtypeStruct((total, LANES), BF),
        ),
        "slot",
        32,
        in_specs=[anywhere] * 5,
        scratch_shapes=[
            pltpu.VMEM((total, width), BF),
            pltpu.VMEM((total, width), BF),
            pltpu.VMEM(sent.shape, BF),
            pltpu.VMEM((width, columns), BF),
            pltpu.SemaphoreType.DMA((7,)),
        ],
        cost_estimate=pl.CostEstimate(
            flops=int(6e9), bytes_accessed=4 * width * columns, transcendentals=0
        ),
    )(got, *w_all)
    first, later = swap(first), swap(later)

    def both(j, n=1):
        theirs, at = (first, j) if j < FIRST else (later, j - FIRST)
        return (
            mine[j * part : (j + n) * part].astype(F32)
            + theirs[at * part : (at + n) * part].astype(F32)
        )

    minus, plus = both(0, 2).astype(BF), both(2).astype(BF)
    minus, plus, pre_grad = lax.optimization_barrier((minus, plus, pre_grad))
    back = call(
        back_kernel,
        jax.ShapeDtypeStruct((rows, width + width // 4 + LANES), BF),
        "back",
        24,
        in_specs=[vmem] * 6,
        scratch_shapes=[pltpu.VMEM((total - rows, width), BF)],
    )(pre_grad, gate_rows, *w_all)
    minus, plus = move(minus, -1), move(plus, 1)
    far_sum = (minus[:part].astype(F32) + both(3)).astype(BF)
    plus = (plus.astype(F32) + both(4)).astype(BF)
    far_sum, plus = move(far_sum, -2), move(plus, 1)
    minus = (far_sum.astype(F32) + minus[part:].astype(F32) + both(5)).astype(BF)
    plus = (plus.astype(F32) + both(6)).astype(BF)
    minus, plus = move(minus, -1), move(plus, 1)
    owned = (minus.astype(F32) + plus.astype(F32) + both(7)).astype(BF)

    back = lax.all_to_all(back, "ep", split_axis=0, concat_axis=0, tiled=True)
    owned, back = lax.optimization_barrier((owned, back))
    token_grad, gate_grad = call(
        join_kernel,
        (
            jax.ShapeDtypeStruct((tok_count, width), BF),
            jax.ShapeDtypeStruct((2, tok_count), BF),
        ),
        "join",
        16,
        in_specs=[smem, smem, vmem, vmem],
    )(*place, back, places)
    owned = owned.reshape(slots, each, columns)
    mixed = lax.all_to_all(owned, "ep", split_axis=0, concat_axis=0, tiled=True)
    weight_grad = call(
        functools.partial(expert_kernel, groups),
        jax.ShapeDtypeStruct((experts, each, columns), F32),
        "experts",
        8,
        in_specs=[smem, vmem],
    )(plan, mixed)
    return token_grad, gate_grad.T, weight_grad


def solution(mesh):
    devices = mesh.devices.reshape(mesh.shape["grp"] // 2, 2, mesh.shape["ep"])
    fine = jax.sharding.Mesh(devices, ("z", "core", "ep"))
    everywhere = P(("z", "core", "ep"), None)
    weight = P("ep", ("z", "core"), None)
    return jax.shard_map(
        local,
        mesh=fine,
        in_specs=(everywhere,) * 4 + (weight, weight, P(), P()),
        out_specs=(everywhere, everywhere, P(None, ("z", "core", "ep"), None)),
        check_vma=False,
    )
```
